256 devices in a mesh: prow: 8 (over y, core), pcol: 32 (over x, z).
Axes of the slice: x: 4, y: 4, z: 8, core: 2. Of those that a mesh axis runs over, the one named last changes fastest.
Arguments:
- matrix: bfloat16 [4096, 32768], P('prow', 'pcol'), may hold values from -4 to 4
- scales: float32 [8, 64], replicated, may hold values from 0.5 to 2
Outputs:
- factored: bfloat16 [4096, 32768], P('prow', 'pcol')
The draws below stay inside these ranges and needn't reach their ends.
All inputs are finite; a program needn't handle non-finite values.
Results may differ from the reference program's by a relative error of at most 0.0046.
Values may be sent and summed in bfloat16 or wider, within the bound.
No kernel may reach another device: no remote copies, remote signals or barrier semaphores. Data moves between devices by JAX's collectives and lax.ppermute only.
A program may use at most 64 MiB of HBM per device.

```python
import math
import jax
import jax.numpy as jnp
from jax import lax

NB = 512
ORDER = 32768
ROWS = 4096
RTILES = 8
TILES = 64
N_PROW = 8
N_PCOL = 32


def draw_matrix(key, part):
    key = jax.random.fold_in(key, 11)
    base = jnp.clip(jax.random.normal(key, (ROWS, ORDER), jnp.float32), -4.0, 4.0)
    row_ids = lax.broadcasted_iota(jnp.int32, (ROWS, 1), 0)
    col_ids = lax.broadcasted_iota(jnp.int32, (1, ORDER), 1)
    in_panel = col_ids < NB
    in_strict = (row_ids < NB) & in_panel & (row_ids > col_ids)
    below = in_panel & (row_ids >= NB)
    factor = jnp.where(in_strict, 0.5 / math.sqrt(NB), jnp.where(below, 1.0 / math.sqrt(NB), 1.0))
    return (base * factor).astype(jnp.bfloat16)


def setup_inputs(seed: int = 0) -> dict:
    streams_of = jax.random.split(jax.random.key(seed), 3)
    return {
        "matrix": draw_matrix(jax.random.fold_in(streams_of[2], 71), 0),
        "scales": jnp.clip(jnp.exp(jax.random.uniform(streams_of[1], (RTILES, TILES), jnp.float32, math.log(0.5), math.log(2.0))), 0.5, 2.0),
    }


def reference(matrix, scales):
    row_count = matrix.shape[0]
    order_size = matrix.shape[1]
    tile_rows_all = row_count // NB
    tile_cols_all = order_size // NB
    row_tiles = tile_rows_all // N_PROW
    col_tiles = tile_cols_all // N_PCOL
    stored_rows = jnp.arange(tile_rows_all, dtype=jnp.int32)
    stored_cols = jnp.arange(tile_cols_all, dtype=jnp.int32)
    row_map = stored_rows % row_tiles * N_PROW + stored_rows // row_tiles
    col_map = stored_cols % col_tiles * N_PCOL + stored_cols // col_tiles
    placed = scales[row_map][:, col_map]
    col_scale = jnp.repeat(placed, NB, axis=1)
    diagonal = matrix[:NB, :NB].astype(jnp.float32) * placed[0, 0]
    lower_unit = jnp.tril(diagonal, -1) + jnp.eye(NB, dtype=jnp.float32)
    head_block = matrix[:NB].astype(jnp.float32) * col_scale[0][None, :]
    upper_rows = lax.linalg.triangular_solve(lower_unit, head_block, left_side=True, lower=True, unit_diagonal=True)
    u_wire = upper_rows.astype(jnp.bfloat16).astype(jnp.float32)

    def one_tile(tile_index):
        rows = lax.dynamic_slice_in_dim(matrix, tile_index * NB, NB, 0).astype(jnp.float32)
        product = jnp.dot(rows[:, :NB].astype(jnp.float32), u_wire.astype(jnp.float32), preferred_element_type=jnp.float32, precision=lax.Precision.HIGHEST)
        product = product * placed[tile_index, 0]
        scale_row = col_scale[tile_index][None, :]
        return ((rows * scale_row - product) / scale_row).astype(jnp.bfloat16)
    updated = lax.map(one_tile, stored_rows).reshape(row_count, order_size)
    head_tiles = (upper_rows / col_scale[0][None, :]).astype(jnp.bfloat16)
    updated = updated.at[:NB].set(head_tiles)
    factored = updated.at[:, :NB].set(matrix[:, :NB])
    return factored
```

```python
import functools

import jax
import jax.numpy as jnp
from jax import lax
from jax.experimental import pallas as pl
from jax.experimental.pallas import tpu as pltpu
from jax.sharding import PartitionSpec as P

NB = 512
BASE = 128
XS = 4
ZS = 8
BF = jnp.bfloat16
F32 = jnp.float32


def bdot(a, b):
    return jnp.dot(a, b, preferred_element_type=F32)


def split3(x):
    high = x.astype(BF)
    rest = x - high.astype(F32)
    mid = rest.astype(BF)
    low = (rest - mid.astype(F32)).astype(BF)
    return high, mid, low


def dot_exact_left(t, x):
    high, mid, low = split3(x)
    return bdot(t, high) + (bdot(t, mid) + bdot(t, low))


def dot_full(a, b):
    ah, am, al = split3(a)
    bh, bm, bl = split3(b)
    return bdot(ah, bh) + (
        (bdot(ah, bm) + bdot(am, bh)) + (bdot(am, bm) + (bdot(ah, bl) + bdot(al, bh)))
    )


def invert_diagonal(tiles, s):
    n = BASE
    r = lax.broadcasted_iota(jnp.int32, (n, n), 0)
    c = lax.broadcasted_iota(jnp.int32, (n, n), 1)
    eye = (r == c).astype(F32)

    def mask(k):
        return ((r // (2 * k)) == (c // (2 * k))) & ((r // k) % 2 == 1) & ((c // k) % 2 == 0)

    first = mask(1)
    inverses = [eye - jnp.where(first, t.astype(F32) * s, 0.0) for t in tiles]
    k = 2
    while k < n:
        at = mask(k)
        inner = [
            dot_exact_left(jnp.where(at, t, jnp.zeros_like(t)), x) * s
            for t, x in zip(tiles, inverses)
        ]
        inverses = [x - dot_full(x, y) for x, y in zip(inverses, inner)]
        k *= 2
    return inverses


def solve_kernel(scales_ref, low_ref, swap_ref, matrix_ref, w0_ref, w1_ref, w2_ref, w3_ref, inv_ref):
    outs = (w0_ref, w1_ref, w2_ref, w3_ref)
    holder = lax.axis_index("pcol") == 0
    prow_at = lax.axis_index("prow")

    @pl.when(jnp.logical_not(holder))
    def _():
        for ref in outs:
            ref[...] = jnp.zeros_like(ref)

    @pl.when(holder)
    def _():
        s = scales_ref[0, 0]
        packed = low_ref[...] + swap_ref[...]
        t = [[None] * 4 for _ in range(4)]
        for j in range(4):
            t[2][j] = packed[:128, 128 * j : 128 * (j + 1)]
            t[3][j] = packed[128:256, 128 * j : 128 * (j + 1)]
        t[0][0], t[0][1] = packed[256:, :128], packed[256:, 128:256]
        t[1][0], t[1][1] = packed[256:, 256:384], packed[256:, 384:]
        x = invert_diagonal([t[i][i] for i in range(4)], s)
        halves = []
        for h in (0, 2):
            off = -dot_full(x[h + 1], dot_exact_left(t[h + 1][h], x[h]) * s)
            top = jnp.concatenate([x[h], jnp.zeros_like(x[h])], 1)
            halves.append(jnp.concatenate([top, jnp.concatenate([off, x[h + 1]], 1)], 0))
        corner = jnp.concatenate(
            [jnp.concatenate([t[2][0], t[2][1]], 1), jnp.concatenate([t[3][0], t[3][1]], 1)], 0
        )
        off = -dot_full(halves[1], dot_exact_left(corner, halves[0]) * s)
        inv_ref[:256, :256] = halves[0]
        inv_ref[:256, 256:] = jnp.zeros_like(off)
        inv_ref[256:, :256] = off
        inv_ref[256:, 256:] = halves[1]
        inverse = inv_ref[...]
        high = inverse.astype(BF)
        low = (inverse - high.astype(F32)).astype(BF)
        for i, ref in enumerate(outs):
            a = matrix_ref[128 * i : 128 * (i + 1), :NB]
            w = (bdot(a, high) + bdot(a, low)).astype(BF)
            ref[...] = jnp.where(prow_at == 0, high[128 * i : 128 * (i + 1)], w)


def solve(scales, low, swap, matrix):
    chunk = jax.ShapeDtypeStruct((128, NB), BF)
    vmem = pl.BlockSpec(memory_space=pltpu.VMEM)
    return pl.pallas_call(
        solve_kernel,
        out_shape=[chunk] * 4,
        in_specs=[pl.BlockSpec(memory_space=pltpu.SMEM), vmem, vmem, vmem],
        out_specs=[vmem] * 4,
        scratch_shapes=[pltpu.VMEM((NB, NB), F32)],
        compiler_params=pltpu.CompilerParams(vmem_limit_bytes=40 * 2**20),
        cost_estimate=pl.CostEstimate(flops=4 * 10**9, bytes_accessed=4 * 2**20, transcendentals=0),
    )(scales, low, swap, matrix)


def update_kernel(
    scales_ref, matrix_ref, mine_ref, swap_ref, extra_ref, q0_ref, q1_ref, q3_ref, q2_ref, out_ref,
    head_ref, w_ref, sems,
):
    prow_at = lax.axis_index("prow")
    pcol_at = lax.axis_index("pcol")
    x_at = pcol_at // ZS

    def place(src, dst, at):
        return pltpu.make_async_copy(src, dst, sems.at[at])

    copies = []
    for at, (ref, shift) in enumerate(((q0_ref, 0), (q1_ref, 3), (q3_ref, 1), (q2_ref, 2))):
        row = pl.multiple_of(lax.rem(x_at + shift, XS) * 128, 128)
        copies.append(place(ref, w_ref.at[pl.ds(row, 128), :], at))
        copies[-1].start()

    @pl.when(prow_at == 0)
    def _():
        head_ref[...] = matrix_ref[...]

    @pl.when(prow_at == 1)
    def _():
        one = place(swap_ref, head_ref.at[:256], 4)
        two = place(extra_ref, head_ref.at[256:], 5)
        one.start()
        two.start()
        one.wait()
        two.wait()

    first = (prow_at == 2) | (prow_at == 4) | (prow_at == 7)

    @pl.when(first)
    def _():
        one = place(mine_ref, head_ref.at[:256], 4)
        two = place(swap_ref, head_ref.at[256:], 5)
        one.start()
        two.start()
        one.wait()
        two.wait()

    @pl.when((prow_at > 1) & jnp.logical_not(first))
    def _():
        one = place(swap_ref, head_ref.at[:256], 4)
        two = place(mine_ref, head_ref.at[256:], 5)
        one.start()
        two.start()
        one.wait()
        two.wait()

    for copy in copies:
        copy.wait()

    for t in range(2):
        cols = slice(NB * t, NB * (t + 1))
        col = NB // 16 * t + pcol_at
        scale = jnp.full((1, NB), scales_ref[prow_at, col], F32)
        factor = (scales_ref[prow_at, 0] * scales_ref[0, col]) / scale
        for i in range(4):
            rows = slice(128 * i, 128 * (i + 1))
            product = bdot(w_ref[rows, :], head_ref[:, cols])
            own = matrix_ref[rows, cols]
            updated = (own.astype(F32) - factor * product).astype(BF)
            result = jnp.where(prow_at == 0, product.astype(BF), updated)
            if t == 0:
                result = jnp.where(pcol_at == 0, own, result)
            out_ref[rows, cols] = result


def update(scales, matrix, heads, chunks):
    vmem = pl.BlockSpec(memory_space=pltpu.VMEM)
    anywhere = pl.BlockSpec(memory_space=pl.ANY)
    return pl.pallas_call(
        update_kernel,
        out_shape=jax.ShapeDtypeStruct(matrix.shape, BF),
        in_specs=[pl.BlockSpec(memory_space=pltpu.SMEM), vmem] + [anywhere] * 7,
        out_specs=vmem,
        scratch_shapes=[
            pltpu.VMEM((NB, 2 * NB), BF),
            pltpu.VMEM((NB, NB), BF),
            pltpu.SemaphoreType.DMA((6,)),
        ],
        compiler_params=pltpu.CompilerParams(vmem_limit_bytes=40 * 2**20),
        cost_estimate=pl.CostEstimate(flops=2**29, bytes_accessed=4 * 2**20, transcendentals=0),
    )(scales, matrix, *heads, *chunks)


def send(value, pairs):
    flat = [
        tuple(p * XS * ZS + x * ZS + z for p, x, z in (source, target)) for source, target in pairs
    ]
    return lax.ppermute(value, ("prow", "pcol"), flat)


def along_prow(value, pairs, columns):
    return send(value, [((a, x, z), (b, x, z)) for a, b in pairs for x, z in columns])


def along_x(value, pairs, depths):
    return send(
        value, [((p, a, z), (p, b, z)) for a, b in pairs for p in range(8) for z in depths]
    )


def along_z(value, pairs):
    return send(
        value, [((p, x, a), (p, x, b)) for a, b in pairs for p in range(8) for x in range(XS)]
    )


def on_device(matrix, scales):
    everywhere = [(x, z) for x in range(XS) for z in range(ZS)]
    corner = [(0, 0)]
    prow_at = lax.axis_index("prow")
    low = jnp.concatenate(
        [
            matrix[256:, :NB],
            jnp.concatenate([matrix[:128, :256], matrix[128:256, :256]], 1),
        ],
        0,
    )
    low = jnp.where((prow_at == 0) & (lax.axis_index("pcol") == 0), low, 0).astype(BF)
    low_y = [along_prow(low, [(0, p)], corner) for p in (4, 2, 6)]
    low = low + low_y[0] + low_y[1] + low_y[2]
    low_swap = along_prow(low, [(0, 1), (2, 3), (4, 5), (6, 7)], corner)

    upper, lower = matrix[:256], matrix[256:]
    to2 = along_prow(upper, [(0, 2)], everywhere)
    to6 = along_prow(lower, [(0, 6)], everywhere)
    to3 = along_prow(lower, [(0, 3)], everywhere)
    to7 = along_prow(upper, [(0, 7)], everywhere)
    mine = to2 + to6
    to45 = along_prow(mine, [(2, 4), (6, 5)], everywhere)
    mine = jnp.where(prow_at == 0, upper, mine + to3 + to7 + to45)
    swap = along_prow(mine, [(0, 1)] + [(p, p ^ 1) for p in range(2, 8)], everywhere)
    extra = along_prow(lower, [(0, 1)], everywhere)

    w = solve(scales, low, low_swap, matrix)
    w_x = [along_x(w[k], [(0, k)], [0]) for k in (2, 1, 3)]
    q = w[0] + w_x[0] + w_x[1] + w_x[2]
    q3, q5 = along_z(q, [(0, 3)]), along_z(q, [(0, 5)])
    q = q + q3 + q5
    up, down = along_z(q, [(0, 1), (3, 4), (5, 6)]), along_z(q, [(0, 7), (3, 2)])
    q = q + up + down
    q2 = along_x(q, [(a, (a + 2) % XS) for a in range(XS)], range(ZS))
    q1 = along_x(q, [(a, (a + 1) % XS) for a in range(XS)], range(ZS))
    q3 = along_x(q, [(a, (a + 3) % XS) for a in range(XS)], range(ZS))
    return update(scales, matrix, (mine, swap, extra), (q, q1, q3, q2))


def solution(mesh):
    placed = (P("prow", "pcol"), P())
    return jax.shard_map(
        on_device, mesh=mesh, in_specs=placed, out_specs=P("prow", "pcol"), check_vma=False
    )
```

```python
import functools

import jax
import jax.numpy as jnp
from jax import lax
from jax.experimental import pallas as pl
from jax.experimental.pallas import tpu as pltpu
from jax.sharding import PartitionSpec as P

NB = 512
BASE = 128
XS = 4
ZS = 8
TILE_COLS = XS * ZS
SOLVE_FLOPS = 0
BF = jnp.bfloat16
F32 = jnp.float32


def bdot(a, b):
    return jnp.dot(a, b, preferred_element_type=F32)


def split3(x):
    high = x.astype(BF)
    rest = x - high.astype(F32)
    mid = rest.astype(BF)
    low = (rest - mid.astype(F32)).astype(BF)
    return high, mid, low


def dot_exact_left(t, x):
    high, mid, low = split3(x)
    return bdot(t, high) + (bdot(t, mid) + bdot(t, low))


def dot_full(a, b):
    ah, am, al = split3(a)
    bh, bm, bl = split3(b)
    return bdot(ah, bh) + (
        (bdot(ah, bm) + bdot(am, bh)) + (bdot(am, bm) + (bdot(ah, bl) + bdot(al, bh)))
    )


def invert_diagonal(tiles, s):
    n = BASE
    r = lax.broadcasted_iota(jnp.int32, (n, n), 0)
    c = lax.broadcasted_iota(jnp.int32, (n, n), 1)
    eye = (r == c).astype(F32)

    def mask(k):
        return ((r // (2 * k)) == (c // (2 * k))) & ((r // k) % 2 == 1) & ((c // k) % 2 == 0)

    first = mask(1)
    inverses = [eye - jnp.where(first, t.astype(F32) * s, 0.0) for t in tiles]
    k = 2
    while k < n:
        at = mask(k)
        inner = [
            dot_exact_left(jnp.where(at, t, jnp.zeros_like(t)), x) * s
            for t, x in zip(tiles, inverses)
        ]
        inverses = [x - dot_full(x, y) for x, y in zip(inverses, inner)]
        k *= 2
    return inverses


def pack_kernel(matrix_ref, out_ref, sems):
    here = (lax.axis_index("prow") == 0) & (lax.axis_index("pcol") == 0)

    @pl.when(jnp.logical_not(here))
    def _():
        out_ref[...] = jnp.zeros_like(out_ref)

    @pl.when(here)
    def _():
        pieces = [(384, 0, 128, 512, 0, 0), (256, 0, 128, 384, 128, 0), (0, 0, 128, 128, 128, 384)]
        pieces += [
            (128 + 64 * i, 128 * j, 64, 128, 256, 256 * j + 128 * i)
            for j in range(2)
            for i in range(2)
        ]
        copies = [
            pltpu.make_async_copy(
                matrix_ref.at[r : r + h, c : c + w], out_ref.at[to_r : to_r + h, to_c : to_c + w], sems.at[at]
            )
            for at, (r, c, h, w, to_r, to_c) in enumerate(pieces)
        ]
        for copy in copies:
            copy.start()
        for copy in copies:
            copy.wait()


def pack(matrix):
    return pl.pallas_call(
        pack_kernel,
        out_shape=pltpu.VMEM((320, NB), BF),
        in_specs=[pl.BlockSpec(memory_space=pl.ANY)],
        out_specs=pl.BlockSpec(memory_space=pltpu.VMEM),
        scratch_shapes=[pltpu.SemaphoreType.DMA((7,))],
        cost_estimate=pl.CostEstimate(flops=0, bytes_accessed=2**19, transcendentals=0),
    )(matrix)


def solve_kernel(
    scales_ref, low_ref, swap_ref, own_ref, w0_ref, w1_ref, w2_ref, w3_ref, inv_ref
):
    outs = (w0_ref, w1_ref, w2_ref, w3_ref)
    holder = lax.axis_index("pcol") == 0
    prow_at = lax.axis_index("prow")

    @pl.when(jnp.logical_not(holder))
    def _():
        for ref in outs:
            ref[...] = jnp.zeros_like(ref)

    @pl.when(holder)
    def _():
        s = scales_ref[0, 0]
        packed = low_ref[...] + swap_ref[...]
        t = [[None] * 4 for _ in range(4)]
        for j in range(4):
            t[3][j] = packed[:128, 128 * j : 128 * (j + 1)]
        for j in range(3):
            t[2][j] = packed[128:256, 128 * j : 128 * (j + 1)]
        t[0][0] = packed[128:256, 384:]
        for j in range(2):
            t[1][j] = jnp.concatenate(
                [packed[256:, 256 * j : 256 * j + 128], packed[256:, 256 * j + 128 : 256 * (j + 1)]], 0
            )
        x = invert_diagonal([t[i][i] for i in range(4)], s)
        halves = []
        for h in (0, 2):
            off = -dot_full(x[h + 1], dot_exact_left(t[h + 1][h], x[h]) * s)
            top = jnp.concatenate([x[h], jnp.zeros_like(x[h])], 1)
            halves.append(jnp.concatenate([top, jnp.concatenate([off, x[h + 1]], 1)], 0))
        corner = jnp.concatenate(
            [jnp.concatenate([t[2][0], t[2][1]], 1), jnp.concatenate([t[3][0], t[3][1]], 1)], 0
        )
        off = -dot_full(halves[1], dot_exact_left(corner, halves[0]) * s)
        inv_ref[:256, :256] = halves[0]
        inv_ref[:256, 256:] = jnp.zeros_like(off)
        inv_ref[256:, :256] = off
        inv_ref[256:, 256:] = halves[1]
        inverse = inv_ref[...]
        high = inverse.astype(BF)
        low = (inverse - high.astype(F32)).astype(BF)
        for i, ref in enumerate(outs):
            a = own_ref[128 * i : 128 * (i + 1), :NB]
            w = (bdot(a, high) + bdot(a, low)).astype(BF)
            ref[...] = jnp.where(prow_at == 0, high[128 * i : 128 * (i + 1)], w)


def solve(scales, low, swap, own):
    chunk = jax.ShapeDtypeStruct((128, NB), BF)
    vmem = pl.BlockSpec(memory_space=pltpu.VMEM)
    return pl.pallas_call(
        solve_kernel,
        out_shape=[chunk] * 4,
        in_specs=[pl.BlockSpec(memory_space=pltpu.SMEM)] + [vmem] * 3,
        out_specs=[vmem] * 4,
        scratch_shapes=[pltpu.VMEM((NB, NB), F32)],
        compiler_params=pltpu.CompilerParams(vmem_limit_bytes=12 * 2**20),
        cost_estimate=pl.CostEstimate(flops=SOLVE_FLOPS, bytes_accessed=0, transcendentals=0),
    )(scales, low, swap, own)


def update_kernel(
    scales_ref, own_ref, held_ref, far_ref, swap_ref, q0_ref, q1_ref, q3_ref, q2_ref, out_ref,
    w_ref, result_ref, sems,
):
    prow_at = lax.axis_index("prow")
    pcol_at = lax.axis_index("pcol")
    for ref, shift in ((q0_ref, 0), (q1_ref, 3), (q3_ref, 1), (q2_ref, 2)):
        row = pl.multiple_of(lax.rem(pcol_at // ZS + shift, XS) * 128, 128)
        w_ref[pl.ds(row, 128), :] = ref[...]
    copies = [
        pltpu.make_async_copy(
            result_ref.at[:, 256 * t : 256 * (t + 1)], out_ref.at[:, 256 * t : 256 * (t + 1)], sems.at[t]
        )
        for t in range(4)
    ]

    def run(head_ref):
        for t in range(4):
            cols = slice(256 * t, 256 * (t + 1))
            col = TILE_COLS * (t // 2) + pcol_at
            scale = jnp.full((1, 256), scales_ref[prow_at, col], F32)
            factor = (scales_ref[prow_at, 0] * scales_ref[0, col]) / scale
            product = bdot(w_ref[...], head_ref[:, cols])
            own = own_ref[:, cols]
            updated = (own.astype(F32) - factor * product).astype(BF)
            result = jnp.where(prow_at == 0, product.astype(BF), updated)
            if t < 2:
                result = jnp.where(pcol_at == 0, own, result)
            result_ref[:, cols] = result
            copies[t].start()

    cases = (
        ((prow_at == 0) | (prow_at == 2) | (prow_at == 6), held_ref),
        ((prow_at == 4) | (prow_at == 5), far_ref),
        ((prow_at == 1) | (prow_at == 3) | (prow_at == 7), swap_ref),
    )
    for here, head_ref in cases:
        pl.when(here)(functools.partial(run, head_ref))
    for copy in copies:
        copy.wait()


def update(scales, own, heads, chunks):
    vmem = pl.BlockSpec(memory_space=pltpu.VMEM)
    return pl.pallas_call(
        update_kernel,
        out_shape=jax.ShapeDtypeStruct((NB, 2 * NB), BF),
        in_specs=[pl.BlockSpec(memory_space=pltpu.SMEM)] + [vmem] * 8,
        out_specs=pl.BlockSpec(memory_space=pl.ANY),
        scratch_shapes=[
            pltpu.VMEM((NB, NB), BF),
            pltpu.VMEM((NB, 2 * NB), BF),
            pltpu.SemaphoreType.DMA((4,)),
        ],
        compiler_params=pltpu.CompilerParams(vmem_limit_bytes=8 * 2**20),
        cost_estimate=pl.CostEstimate(flops=2**29, bytes_accessed=4 * 2**20, transcendentals=0),
    )(scales, own, *heads, *chunks)


def send(value, pairs):
    flat = [
        tuple(p * XS * ZS + x * ZS + z for p, x, z in (source, target)) for source, target in pairs
    ]
    return lax.ppermute(value, ("prow", "pcol"), flat)


def along_prow(value, pairs, columns):
    return send(value, [((a, x, z), (b, x, z)) for a, b in pairs for x, z in columns])


def along_x(value, pairs, depths):
    return send(
        value, [((p, a, z), (p, b, z)) for a, b in pairs for p in range(8) for z in depths]
    )


def along_z(value, pairs):
    return send(
        value, [((p, x, a), (p, x, b)) for a, b in pairs for p in range(8) for x in range(XS)]
    )


def on_device(matrix, scales):
    everywhere = [(x, z) for x in range(XS) for z in range(ZS)]
    corner = [(0, 0)]
    prow_at = lax.axis_index("prow")
    low = pack(matrix)
    low_y = [along_prow(low, [(0, p)], corner) for p in (4, 2, 6)]
    own, *low_y = lax.optimization_barrier((matrix, *low_y))
    low = low + low_y[0] + low_y[1] + low_y[2]
    low_swap = along_prow(low, [(p, p ^ 1) for p in range(8)], corner)
    low = jnp.where(prow_at % 2 == 0, low, 0).astype(BF)
    y2 = along_prow(own, [(0, 2)], everywhere)
    y6 = along_prow(own, [(0, 6)], everywhere)

    w = solve(scales, low, low_swap, matrix)
    w_x = [along_x(w[k], [(0, k)], [0]) for k in (2, 1, 3)]
    q = w[0] + w_x[0] + w_x[1] + w_x[2]
    q3, q5 = along_z(q, [(0, 3)]), along_z(q, [(0, 5)])
    q = q + q3 + q5
    q, y2, y6 = lax.optimization_barrier((q, y2, y6))
    held = jnp.where(prow_at == 0, matrix, y2 + y6)
    far = along_prow(held, [(2, 4), (6, 5)], everywhere)
    swap = along_prow(held, [(0, 1), (2, 3), (6, 7)], everywhere)
    up_z, down_z = along_z(q, [(0, 1), (3, 4), (5, 6)]), along_z(q, [(0, 7), (3, 2)])
    q = q + up_z + down_z
    q2 = along_x(q, [(a, (a + 2) % XS) for a in range(XS)], range(ZS))
    q1 = along_x(q, [(a, (a + 1) % XS) for a in range(XS)], range(ZS))
    q3 = along_x(q, [(a, (a + 3) % XS) for a in range(XS)], range(ZS))
    return update(scales, matrix, (held, far, swap), (q, q1, q3, q2))


def solution(mesh):
    placed = (P("prow", "pcol"), P())
    return jax.shard_map(
        on_device, mesh=mesh, in_specs=placed, out_specs=P("prow", "pcol"), check_vma=False
    )
```

```python
import functools

import jax
import jax.numpy as jnp
from jax import lax
from jax.experimental import pallas as pl
from jax.experimental.pallas import tpu as pltpu
from jax.sharding import PartitionSpec as P

NB = 512
BASE = 128
XS = 4
ZS = 8
TILE_COLS = XS * ZS
SOLVE_FLOPS = 0
BF = jnp.bfloat16
F32 = jnp.float32


def bdot(a, b):
    return jnp.dot(a, b, preferred_element_type=F32)


def split3(x):
    high = x.astype(BF)
    rest = x - high.astype(F32)
    mid = rest.astype(BF)
    low = (rest - mid.astype(F32)).astype(BF)
    return high, mid, low


def dot_exact_left(t, x):
    high, mid, low = split3(x)
    return bdot(t, high) + (bdot(t, mid) + bdot(t, low))


def dot_full(a, b):
    ah, am, al = split3(a)
    bh, bm, bl = split3(b)
    return bdot(ah, bh) + (
        (bdot(ah, bm) + bdot(am, bh)) + (bdot(am, bm) + (bdot(ah, bl) + bdot(al, bh)))
    )


def invert_diagonal(tiles, s):
    n = BASE
    r = lax.broadcasted_iota(jnp.int32, (n, n), 0)
    c = lax.broadcasted_iota(jnp.int32, (n, n), 1)
    eye = (r == c).astype(F32)

    def mask(k):
        return ((r // (2 * k)) == (c // (2 * k))) & ((r // k) % 2 == 1) & ((c // k) % 2 == 0)

    first = mask(1)
    inverses = [eye - jnp.where(first, t.astype(F32) * s, 0.0) for t in tiles]
    k = 2
    while k < n:
        at = mask(k)
        inner = [
            dot_exact_left(jnp.where(at, t, jnp.zeros_like(t)), x) * s
            for t, x in zip(tiles, inverses)
        ]
        inverses = [x - dot_full(x, y) for x, y in zip(inverses, inner)]
        k *= 2
    return inverses


def pack_kernel(matrix_ref, out_ref, sems):
    here = (lax.axis_index("prow") == 0) & (lax.axis_index("pcol") == 0)

    @pl.when(jnp.logical_not(here))
    def _():
        out_ref[...] = jnp.zeros_like(out_ref)

    @pl.when(here)
    def _():
        pieces = [(384, 0, 128, 512, 0, 0), (256, 0, 128, 384, 128, 0), (0, 0, 128, 128, 128, 384)]
        pieces += [
            (128 + 64 * i, 128 * j, 64, 128, 256, 256 * j + 128 * i)
            for j in range(2)
            for i in range(2)
        ]
        copies = [
            pltpu.make_async_copy(
                matrix_ref.at[r : r + h, c : c + w], out_ref.at[to_r : to_r + h, to_c : to_c + w], sems.at[at]
            )
            for at, (r, c, h, w, to_r, to_c) in enumerate(pieces)
        ]
        for copy in copies:
            copy.start()
        for copy in copies:
            copy.wait()


def pack(matrix):
    return pl.pallas_call(
        pack_kernel,
        out_shape=pltpu.VMEM((320, NB), BF),
        in_specs=[pl.BlockSpec(memory_space=pl.ANY)],
        out_specs=pl.BlockSpec(memory_space=pltpu.VMEM),
        scratch_shapes=[pltpu.SemaphoreType.DMA((7,))],
        cost_estimate=pl.CostEstimate(flops=0, bytes_accessed=2**19, transcendentals=0),
    )(matrix)


def solve_kernel(
    scales_ref, low_ref, swap_ref, own_ref, w0_ref, w1_ref, w2_ref, w3_ref, inv_ref
):
    outs = (w0_ref, w1_ref, w2_ref, w3_ref)
    holder = lax.axis_index("pcol") == 0
    prow_at = lax.axis_index("prow")

    @pl.when(jnp.logical_not(holder))
    def _():
        for ref in outs:
            ref[...] = jnp.zeros_like(ref)

    @pl.when(holder)
    def _():
        s = scales_ref[0, 0]
        packed = low_ref[...] + swap_ref[...]
        t = [[None] * 4 for _ in range(4)]
        for j in range(4):
            t[3][j] = packed[:128, 128 * j : 128 * (j + 1)]
        for j in range(3):
            t[2][j] = packed[128:256, 128 * j : 128 * (j + 1)]
        t[0][0] = packed[128:256, 384:]
        for j in range(2):
            t[1][j] = jnp.concatenate(
                [packed[256:, 256 * j : 256 * j + 128], packed[256:, 256 * j + 128 : 256 * (j + 1)]], 0
            )
        x = invert_diagonal([t[i][i] for i in range(4)], s)
        halves = []
        for h in (0, 2):
            off = -dot_full(x[h + 1], dot_exact_left(t[h + 1][h], x[h]) * s)
            top = jnp.concatenate([x[h], jnp.zeros_like(x[h])], 1)
            halves.append(jnp.concatenate([top, jnp.concatenate([off, x[h + 1]], 1)], 0))
        corner = jnp.concatenate(
            [jnp.concatenate([t[2][0], t[2][1]], 1), jnp.concatenate([t[3][0], t[3][1]], 1)], 0
        )
        off = -dot_full(halves[1], dot_exact_left(corner, halves[0]) * s)
        inv_ref[:256, :256] = halves[0]
        inv_ref[:256, 256:] = jnp.zeros_like(off)
        inv_ref[256:, :256] = off
        inv_ref[256:, 256:] = halves[1]
        inverse = inv_ref[...]
        high = inverse.astype(BF)
        low = (inverse - high.astype(F32)).astype(BF)
        for i, ref in enumerate(outs):
            a = own_ref[128 * i : 128 * (i + 1), :NB]
            w = (bdot(a, high) + bdot(a, low)).astype(BF)
            ref[...] = jnp.where(prow_at == 0, high[128 * i : 128 * (i + 1)], w)


def solve(scales, low, swap, own):
    chunk = jax.ShapeDtypeStruct((128, NB), BF)
    vmem = pl.BlockSpec(memory_space=pltpu.VMEM)
    return pl.pallas_call(
        solve_kernel,
        out_shape=[chunk] * 4,
        in_specs=[pl.BlockSpec(memory_space=pltpu.SMEM)] + [vmem] * 3,
        out_specs=[vmem] * 4,
        scratch_shapes=[pltpu.VMEM((NB, NB), F32)],
        compiler_params=pltpu.CompilerParams(vmem_limit_bytes=12 * 2**20),
        cost_estimate=pl.CostEstimate(flops=SOLVE_FLOPS, bytes_accessed=0, transcendentals=0),
    )(scales, low, swap, own)


def merge_kernel(held_ref, far_ref, out_ref, sem):
    del held_ref

    @pl.when(lax.axis_index("prow") == 4)
    def _():
        copy = pltpu.make_async_copy(far_ref, out_ref, sem)
        copy.start()
        copy.wait()


def merge(held, far):
    vmem = pl.BlockSpec(memory_space=pltpu.VMEM)
    return pl.pallas_call(
        merge_kernel,
        out_shape=pltpu.VMEM(held.shape, BF),
        in_specs=[vmem, pl.BlockSpec(memory_space=pl.ANY)],
        out_specs=vmem,
        scratch_shapes=[pltpu.SemaphoreType.DMA],
        input_output_aliases={0: 0},
        compiler_params=pltpu.CompilerParams(vmem_limit_bytes=2**20),
        cost_estimate=pl.CostEstimate(flops=0, bytes_accessed=0, transcendentals=0),
    )(held, far)


def update_kernel(
    scales_ref, own_ref, even_ref, odd_ref, q0_ref, q1_ref, q3_ref, q2_ref, out_ref,
    w_ref, result_ref, sems,
):
    prow_at = lax.axis_index("prow")
    pcol_at = lax.axis_index("pcol")
    for ref, shift in ((q0_ref, 0), (q1_ref, 3), (q3_ref, 1), (q2_ref, 2)):
        row = pl.multiple_of(lax.rem(pcol_at // ZS + shift, XS) * 128, 128)
        w_ref[pl.ds(row, 128), :] = ref[...]
    copies = [
        pltpu.make_async_copy(
            result_ref.at[:, 256 * t : 256 * (t + 1)], out_ref.at[:, 256 * t : 256 * (t + 1)], sems.at[t]
        )
        for t in range(4)
    ]

    def run(head_ref):
        for t in range(4):
            cols = slice(256 * t, 256 * (t + 1))
            col = TILE_COLS * (t // 2) + pcol_at
            scale = jnp.full((1, 256), scales_ref[prow_at, col], F32)
            factor = (scales_ref[prow_at, 0] * scales_ref[0, col]) / scale
            product = bdot(w_ref[...], head_ref[:, cols])
            own = own_ref[:, cols]
            updated = (own.astype(F32) - factor * product).astype(BF)
            result = jnp.where(prow_at == 0, product.astype(BF), updated)
            if t < 2:
                result = jnp.where(pcol_at == 0, own, result)
            result_ref[:, cols] = result
            copies[t].start()

    even = lax.rem(prow_at, 2) == 0
    cases = ((even, even_ref), (jnp.logical_not(even), odd_ref))
    for here, head_ref in cases:
        pl.when(here)(functools.partial(run, head_ref))
    for copy in copies:
        copy.wait()


def update(scales, own, heads, chunks):
    vmem = pl.BlockSpec(memory_space=pltpu.VMEM)
    return pl.pallas_call(
        update_kernel,
        out_shape=jax.ShapeDtypeStruct((NB, 2 * NB), BF),
        in_specs=[pl.BlockSpec(memory_space=pltpu.SMEM)] + [vmem] * 7,
        out_specs=pl.BlockSpec(memory_space=pl.ANY),
        scratch_shapes=[
            pltpu.VMEM((NB, NB), BF),
            pltpu.VMEM((NB, 2 * NB), BF),
            pltpu.SemaphoreType.DMA((4,)),
        ],
        compiler_params=pltpu.CompilerParams(vmem_limit_bytes=8 * 2**20),
        cost_estimate=pl.CostEstimate(flops=2**29, bytes_accessed=4 * 2**20, transcendentals=0),
    )(scales, own, *heads, *chunks)


def send(value, pairs):
    flat = [
        tuple(p * XS * ZS + x * ZS + z for p, x, z in (source, target)) for source, target in pairs
    ]
    return lax.ppermute(value, ("prow", "pcol"), flat)


def along_prow(value, pairs, columns):
    return send(value, [((a, x, z), (b, x, z)) for a, b in pairs for x, z in columns])


def along_x(value, pairs, depths):
    return send(
        value, [((p, a, z), (p, b, z)) for a, b in pairs for p in range(8) for z in depths]
    )


def along_z(value, pairs):
    return send(
        value, [((p, x, a), (p, x, b)) for a, b in pairs for p in range(8) for x in range(XS)]
    )


def on_device(matrix, scales):
    everywhere = [(x, z) for x in range(XS) for z in range(ZS)]
    corner = [(0, 0)]
    prow_at = lax.axis_index("prow")
    low = pack(matrix)
    low_y = [along_prow(low, [(0, p)], corner) for p in (4, 2, 6)]
    own, *low_y = lax.optimization_barrier((matrix, *low_y))
    low = low + low_y[0] + low_y[1] + low_y[2]
    low_swap = along_prow(low, [(p, p ^ 1) for p in range(8)], corner)
    low = jnp.where(prow_at % 2 == 0, low, 0).astype(BF)
    y2 = along_prow(own, [(0, 2)], everywhere)
    y6 = along_prow(own, [(0, 6)], everywhere)
    y4 = along_prow(own, [(0, 4)], everywhere)

    w = solve(scales, low, low_swap, matrix)
    w_x = [along_x(w[k], [(0, k)], [0]) for k in (2, 1, 3)]
    q = w[0] + w_x[0] + w_x[1] + w_x[2]
    q3, q5 = along_z(q, [(0, 3)]), along_z(q, [(0, 5)])
    q = q + q3 + q5
    q, y2, y6 = lax.optimization_barrier((q, y2, y6))
    even = jnp.where(prow_at == 0, matrix, y2 + y6)
    up_z, down_z = along_z(q, [(0, 1), (3, 4), (5, 6)]), along_z(q, [(0, 7), (3, 2)])
    q = q + up_z + down_z
    q, even, y4 = lax.optimization_barrier((q, even, y4))
    even = merge(even, y4)
    odd = along_prow(even, [(0, 1), (2, 3), (4, 5), (6, 7)], everywhere)
    q2 = along_x(q, [(a, (a + 2) % XS) for a in range(XS)], range(ZS))
    q1 = along_x(q, [(a, (a + 1) % XS) for a in range(XS)], range(ZS))
    q3 = along_x(q, [(a, (a + 3) % XS) for a in range(XS)], range(ZS))
    return update(scales, matrix, (even, odd), (q, q1, q3, q2))


def solution(mesh):
    placed = (P("prow", "pcol"), P())
    return jax.shard_map(
        on_device, mesh=mesh, in_specs=placed, out_specs=P("prow", "pcol"), check_vma=False
    )
```

```python
import functools

import jax
import jax.numpy as jnp
from jax import lax
from jax.experimental import pallas as pl
from jax.experimental.pallas import tpu as pltpu
from jax.sharding import PartitionSpec as P

NB = 512
BASE = 128
XS = 4
ZS = 8
TILE_COLS = XS * ZS
SOLVE_FLOPS = 0
BF = jnp.bfloat16
F32 = jnp.float32


def bdot(a, b):
    return jnp.dot(a, b, preferred_element_type=F32)


def split3(x):
    high = x.astype(BF)
    rest = x - high.astype(F32)
    mid = rest.astype(BF)
    low = (rest - mid.astype(F32)).astype(BF)
    return high, mid, low


def dot_exact_left(t, x):
    high, mid, low = split3(x)
    return bdot(t, high) + (bdot(t, mid) + bdot(t, low))


def dot_full(a, b):
    ah, am, al = split3(a)
    bh, bm, bl = split3(b)
    return bdot(ah, bh) + (
        (bdot(ah, bm) + bdot(am, bh)) + (bdot(am, bm) + (bdot(ah, bl) + bdot(al, bh)))
    )


def invert_diagonal(tiles, s):
    n = BASE
    r = lax.broadcasted_iota(jnp.int32, (n, n), 0)
    c = lax.broadcasted_iota(jnp.int32, (n, n), 1)
    eye = (r == c).astype(F32)

    def mask(k):
        return ((r // (2 * k)) == (c // (2 * k))) & ((r // k) % 2 == 1) & ((c // k) % 2 == 0)

    first = mask(1)
    inverses = [eye - jnp.where(first, t.astype(F32) * s, 0.0) for t in tiles]
    k = 2
    while k < n:
        at = mask(k)
        inner = [
            dot_exact_left(jnp.where(at, t, jnp.zeros_like(t)), x) * s
            for t, x in zip(tiles, inverses)
        ]
        inverses = [x - dot_full(x, y) for x, y in zip(inverses, inner)]
        k *= 2
    return inverses


def pack_kernel(matrix_ref, out_ref, sems):
    here = (lax.axis_index("prow") == 0) & (lax.axis_index("pcol") == 0)

    @pl.when(jnp.logical_not(here))
    def _():
        out_ref[...] = jnp.zeros_like(out_ref)

    @pl.when(here)
    def _():
        pieces = [(384, 0, 128, 512, 0, 0), (256, 0, 128, 384, 128, 0), (0, 0, 128, 128, 128, 384)]
        pieces += [
            (128 + 64 * i, 128 * j, 64, 128, 256, 256 * j + 128 * i)
            for j in range(2)
            for i in range(2)
        ]
        copies = [
            pltpu.make_async_copy(
                matrix_ref.at[r : r + h, c : c + w], out_ref.at[to_r : to_r + h, to_c : to_c + w], sems.at[at]
            )
            for at, (r, c, h, w, to_r, to_c) in enumerate(pieces)
        ]
        for copy in copies:
            copy.start()
        for copy in copies:
            copy.wait()


def pack(matrix):
    return pl.pallas_call(
        pack_kernel,
        out_shape=pltpu.VMEM((320, NB), BF),
        in_specs=[pl.BlockSpec(memory_space=pl.ANY)],
        out_specs=pl.BlockSpec(memory_space=pltpu.VMEM),
        scratch_shapes=[pltpu.SemaphoreType.DMA((7,))],
        cost_estimate=pl.CostEstimate(flops=0, bytes_accessed=2**19, transcendentals=0),
    )(matrix)


def solve_kernel(
    scales_ref, low_ref, swap_ref, own_ref, w0_ref, w1_ref, w2_ref, w3_ref, inv_ref
):
    outs = (w0_ref, w1_ref, w2_ref, w3_ref)
    holder = lax.axis_index("pcol") == 0
    prow_at = lax.axis_index("prow")

    @pl.when(jnp.logical_not(holder))
    def _():
        for ref in outs:
            ref[...] = jnp.zeros_like(ref)

    @pl.when(holder)
    def _():
        s = scales_ref[0, 0]
        packed = low_ref[...] + swap_ref[...]
        t = [[None] * 4 for _ in range(4)]
        for j in range(4):
            t[3][j] = packed[:128, 128 * j : 128 * (j + 1)]
        for j in range(3):
            t[2][j] = packed[128:256, 128 * j : 128 * (j + 1)]
        t[0][0] = packed[128:256, 384:]
        for j in range(2):
            t[1][j] = jnp.concatenate(
                [packed[256:, 256 * j : 256 * j + 128], packed[256:, 256 * j + 128 : 256 * (j + 1)]], 0
            )
        x = invert_diagonal([t[i][i] for i in range(4)], s)
        halves = []
        for h in (0, 2):
            off = -dot_full(x[h + 1], dot_exact_left(t[h + 1][h], x[h]) * s)
            top = jnp.concatenate([x[h], jnp.zeros_like(x[h])], 1)
            halves.append(jnp.concatenate([top, jnp.concatenate([off, x[h + 1]], 1)], 0))
        corner = jnp.concatenate(
            [jnp.concatenate([t[2][0], t[2][1]], 1), jnp.concatenate([t[3][0], t[3][1]], 1)], 0
        )
        off = -dot_full(halves[1], dot_exact_left(corner, halves[0]) * s)
        inv_ref[:256, :256] = halves[0]
        inv_ref[:256, 256:] = jnp.zeros_like(off)
        inv_ref[256:, :256] = off
        inv_ref[256:, 256:] = halves[1]
        inverse = inv_ref[...]
        high = inverse.astype(BF)
        low = (inverse - high.astype(F32)).astype(BF)
        for i, ref in enumerate(outs):
            a = own_ref[128 * i : 128 * (i + 1), :NB]
            w = (bdot(a, high) + bdot(a, low)).astype(BF)
            ref[...] = jnp.where(prow_at == 0, high[128 * i : 128 * (i + 1)], w)


def solve(scales, low, swap, own):
    chunk = jax.ShapeDtypeStruct((128, NB), BF)
    vmem = pl.BlockSpec(memory_space=pltpu.VMEM)
    return pl.pallas_call(
        solve_kernel,
        out_shape=[chunk] * 4,
        in_specs=[pl.BlockSpec(memory_space=pltpu.SMEM)] + [vmem] * 3,
        out_specs=[vmem] * 4,
        scratch_shapes=[pltpu.VMEM((NB, NB), F32)],
        compiler_params=pltpu.CompilerParams(vmem_limit_bytes=12 * 2**20),
        cost_estimate=pl.CostEstimate(flops=SOLVE_FLOPS, bytes_accessed=0, transcendentals=0),
    )(scales, low, swap, own)


def merge_kernel(y2_ref, matrix_ref, y4_ref, y6_ref, out_ref, sem):
    del y2_ref
    prow_at = lax.axis_index("prow")
    for at, ref in ((0, matrix_ref), (4, y4_ref), (6, y6_ref)):

        @pl.when(prow_at == at)
        def _():
            copy = pltpu.make_async_copy(ref, out_ref, sem)
            copy.start()
            copy.wait()


def merge(y2, blocks):
    vmem = pl.BlockSpec(memory_space=pltpu.VMEM)
    return pl.pallas_call(
        merge_kernel,
        out_shape=pltpu.VMEM(y2.shape, BF),
        in_specs=[vmem] + [pl.BlockSpec(memory_space=pl.ANY)] * 3,
        out_specs=vmem,
        scratch_shapes=[pltpu.SemaphoreType.DMA],
        input_output_aliases={0: 0},
        compiler_params=pltpu.CompilerParams(vmem_limit_bytes=2**20),
        cost_estimate=pl.CostEstimate(flops=0, bytes_accessed=0, transcendentals=0),
    )(y2, *blocks)


def update_kernel(
    scales_ref, own_ref, even_ref, odd_ref, q0_ref, q1_ref, q3_ref, q2_ref, out_ref,
    w_ref, result_ref, sems,
):
    prow_at = lax.axis_index("prow")
    pcol_at = lax.axis_index("pcol")
    for ref, shift in ((q0_ref, 0), (q1_ref, 3), (q3_ref, 1), (q2_ref, 2)):
        row = pl.multiple_of(lax.rem(pcol_at // ZS + shift, XS) * 128, 128)
        w_ref[pl.ds(row, 128), :] = ref[...]
    copies = [
        pltpu.make_async_copy(
            result_ref.at[:, 256 * t : 256 * (t + 1)], out_ref.at[:, 256 * t : 256 * (t + 1)], sems.at[t]
        )
        for t in range(4)
    ]

    def run(head_ref):
        for t in range(4):
            cols = slice(256 * t, 256 * (t + 1))
            col = TILE_COLS * (t // 2) + pcol_at
            scale = jnp.full((1, 256), scales_ref[prow_at, col], F32)
            factor = (scales_ref[prow_at, 0] * scales_ref[0, col]) / scale
            product = bdot(w_ref[...], head_ref[:, cols])
            own = own_ref[:, cols]
            updated = (own.astype(F32) - factor * product).astype(BF)
            result = jnp.where(prow_at == 0, product.astype(BF), updated)
            if t < 2:
                result = jnp.where(pcol_at == 0, own, result)
            result_ref[:, cols] = result
            copies[t].start()

    even = lax.rem(prow_at, 2) == 0
    cases = ((even, even_ref), (jnp.logical_not(even), odd_ref))
    for here, head_ref in cases:
        pl.when(here)(functools.partial(run, head_ref))
    for copy in copies:
        copy.wait()


def update(scales, own, heads, chunks):
    vmem = pl.BlockSpec(memory_space=pltpu.VMEM)
    return pl.pallas_call(
        update_kernel,
        out_shape=jax.ShapeDtypeStruct((NB, 2 * NB), BF),
        in_specs=[pl.BlockSpec(memory_space=pltpu.SMEM)] + [vmem] * 7,
        out_specs=pl.BlockSpec(memory_space=pl.ANY),
        scratch_shapes=[
            pltpu.VMEM((NB, NB), BF),
            pltpu.VMEM((NB, 2 * NB), BF),
            pltpu.SemaphoreType.DMA((4,)),
        ],
        compiler_params=pltpu.CompilerParams(vmem_limit_bytes=8 * 2**20),
        cost_estimate=pl.CostEstimate(flops=2**29, bytes_accessed=4 * 2**20, transcendentals=0),
    )(scales, own, *heads, *chunks)


def send(value, pairs):
    flat = [
        tuple(p * XS * ZS + x * ZS + z for p, x, z in (source, target)) for source, target in pairs
    ]
    return lax.ppermute(value, ("prow", "pcol"), flat)


def along_prow(value, pairs, columns):
    return send(value, [((a, x, z), (b, x, z)) for a, b in pairs for x, z in columns])


def along_x(value, pairs, depths):
    return send(
        value, [((p, a, z), (p, b, z)) for a, b in pairs for p in range(8) for z in depths]
    )


def along_z(value, pairs):
    return send(
        value, [((p, x, a), (p, x, b)) for a, b in pairs for p in range(8) for x in range(XS)]
    )


def on_device(matrix, scales):
    everywhere = [(x, z) for x in range(XS) for z in range(ZS)]
    corner = [(0, 0)]
    prow_at = lax.axis_index("prow")
    low = pack(matrix)
    low_y = [along_prow(low, [(0, p)], corner) for p in (2, 6, 4)]
    own, *low_y = lax.optimization_barrier((matrix, *low_y))
    low = low + low_y[0] + low_y[1] + low_y[2]
    low_swap = along_prow(low, [(p, p ^ 1) for p in range(8)], corner)
    low = jnp.where(prow_at % 2 == 0, low, 0).astype(BF)
    y2 = along_prow(own, [(0, 2)], everywhere)
    y6 = along_prow(own, [(0, 6)], everywhere)
    y4 = along_prow(own, [(0, 4)], everywhere)

    w = solve(scales, low, low_swap, matrix)
    w_x = [along_x(w[k], [(0, k)], [0]) for k in (2, 1, 3)]
    q = w[0] + w_x[0] + w_x[1] + w_x[2]
    q3, q5 = along_z(q, [(0, 3)]), along_z(q, [(0, 5)])
    q = q + q3 + q5
    q, y2, y6 = lax.optimization_barrier((q, y2, y6))
    up_z, down_z = along_z(q, [(0, 1), (3, 4), (5, 6)]), along_z(q, [(0, 7), (3, 2)])
    q = q + up_z + down_z
    q, y2, y4, y6 = lax.optimization_barrier((q, y2, y4, y6))
    even = merge(y2, (matrix, y4, y6))
    odd = along_prow(even, [(0, 1), (2, 3), (4, 5), (6, 7)], everywhere)
    q2 = along_x(q, [(a, (a + 2) % XS) for a in range(XS)], range(ZS))
    q1 = along_x(q, [(a, (a + 1) % XS) for a in range(XS)], range(ZS))
    q3 = along_x(q, [(a, (a + 3) % XS) for a in range(XS)], range(ZS))
    return update(scales, matrix, (even, odd), (q, q1, q3, q2))


def solution(mesh):
    placed = (P("prow", "pcol"), P())
    return jax.shard_map(
        on_device, mesh=mesh, in_specs=placed, out_specs=P("prow", "pcol"), check_vma=False
    )
```

```python
import functools

import jax
import jax.numpy as jnp
from jax import lax
from jax.experimental import pallas as pl
from jax.experimental.pallas import tpu as pltpu
from jax.sharding import PartitionSpec as P

NB = 512
BASE = 128
XS = 4
ZS = 8
TILE_COLS = XS * ZS
SOLVE_FLOPS = 0
BF = jnp.bfloat16
F32 = jnp.float32


def bdot(a, b):
    return jnp.dot(a, b, preferred_element_type=F32)


def split3(x):
    high = x.astype(BF)
    rest = x - high.astype(F32)
    mid = rest.astype(BF)
    low = (rest - mid.astype(F32)).astype(BF)
    return high, mid, low


def dot_exact_left(t, x):
    high, mid, low = split3(x)
    return bdot(t, high) + (bdot(t, mid) + bdot(t, low))


def dot_full(a, b):
    ah, am, al = split3(a)
    bh, bm, bl = split3(b)
    return bdot(ah, bh) + (
        (bdot(ah, bm) + bdot(am, bh)) + (bdot(am, bm) + (bdot(ah, bl) + bdot(al, bh)))
    )


def invert_diagonal(tiles, s):
    n = BASE
    r = lax.broadcasted_iota(jnp.int32, (n, n), 0)
    c = lax.broadcasted_iota(jnp.int32, (n, n), 1)
    eye = (r == c).astype(F32)

    def mask(k):
        return ((r // (2 * k)) == (c // (2 * k))) & ((r // k) % 2 == 1) & ((c // k) % 2 == 0)

    first = mask(1)
    inverses = [eye - jnp.where(first, t.astype(F32) * s, 0.0) for t in tiles]
    k = 2
    while k < n:
        at = mask(k)
        inner = [
            dot_exact_left(jnp.where(at, t, jnp.zeros_like(t)), x) * s
            for t, x in zip(tiles, inverses)
        ]
        inverses = [x - dot_full(x, y) for x, y in zip(inverses, inner)]
        k *= 2
    return inverses


def pack_kernel(matrix_ref, out_ref, sems):
    here = (lax.axis_index("prow") == 0) & (lax.axis_index("pcol") == 0)

    @pl.when(jnp.logical_not(here))
    def _():
        out_ref[...] = jnp.zeros_like(out_ref)

    @pl.when(here)
    def _():
        pieces = [(384, 0, 128, 512, 0, 0), (256, 0, 128, 384, 128, 0), (0, 0, 128, 128, 128, 384)]
        pieces += [
            (128 + 64 * i, 128 * j, 64, 128, 256, 256 * j + 128 * i)
            for j in range(2)
            for i in range(2)
        ]
        copies = [
            pltpu.make_async_copy(
                matrix_ref.at[r : r + h, c : c + w], out_ref.at[to_r : to_r + h, to_c : to_c + w], sems.at[at]
            )
            for at, (r, c, h, w, to_r, to_c) in enumerate(pieces)
        ]
        for copy in copies:
            copy.start()
        for copy in copies:
            copy.wait()


def pack(matrix):
    return pl.pallas_call(
        pack_kernel,
        out_shape=pltpu.VMEM((320, NB), BF),
        in_specs=[pl.BlockSpec(memory_space=pl.ANY)],
        out_specs=pl.BlockSpec(memory_space=pltpu.VMEM),
        scratch_shapes=[pltpu.SemaphoreType.DMA((7,))],
        cost_estimate=pl.CostEstimate(flops=0, bytes_accessed=2**19, transcendentals=0),
    )(matrix)


def solve_kernel(
    scales_ref, low_ref, swap_ref, own_ref, w0_ref, w1_ref, w2_ref, w3_ref, inv_ref
):
    outs = (w0_ref, w1_ref, w2_ref, w3_ref)
    holder = lax.axis_index("pcol") == 0
    prow_at = lax.axis_index("prow")

    @pl.when(jnp.logical_not(holder))
    def _():
        for ref in outs:
            ref[...] = jnp.zeros_like(ref)

    @pl.when(holder)
    def _():
        s = scales_ref[:1, :1]
        packed = low_ref[...] + swap_ref[...]
        t = [[None] * 4 for _ in range(4)]
        for j in range(4):
            t[3][j] = packed[:128, 128 * j : 128 * (j + 1)]
        for j in range(3):
            t[2][j] = packed[128:256, 128 * j : 128 * (j + 1)]
        t[0][0] = packed[128:256, 384:]
        for j in range(2):
            t[1][j] = jnp.concatenate(
                [packed[256:, 256 * j : 256 * j + 128], packed[256:, 256 * j + 128 : 256 * (j + 1)]], 0
            )
        x = invert_diagonal([t[i][i] for i in range(4)], s)
        halves = []
        for h in (0, 2):
            off = -dot_full(x[h + 1], dot_exact_left(t[h + 1][h], x[h]) * s)
            top = jnp.concatenate([x[h], jnp.zeros_like(x[h])], 1)
            halves.append(jnp.concatenate([top, jnp.concatenate([off, x[h + 1]], 1)], 0))
        corner = jnp.concatenate(
            [jnp.concatenate([t[2][0], t[2][1]], 1), jnp.concatenate([t[3][0], t[3][1]], 1)], 0
        )
        off = -dot_full(halves[1], dot_exact_left(corner, halves[0]) * s)
        inv_ref[:256, :256] = halves[0]
        inv_ref[:256, 256:] = jnp.zeros_like(off)
        inv_ref[256:, :256] = off
        inv_ref[256:, 256:] = halves[1]
        inverse = inv_ref[...]
        high = inverse.astype(BF)
        low = (inverse - high.astype(F32)).astype(BF)
        for i, ref in enumerate(outs):
            a = own_ref[128 * i : 128 * (i + 1), :NB]
            w = (bdot(a, high) + bdot(a, low)).astype(BF)
            ref[...] = jnp.where(prow_at == 0, high[128 * i : 128 * (i + 1)], w)


def solve(scales, low, swap, own):
    chunk = jax.ShapeDtypeStruct((128, NB), BF)
    vmem = pl.BlockSpec(memory_space=pltpu.VMEM)
    return pl.pallas_call(
        solve_kernel,
        out_shape=[chunk] * 4,
        in_specs=[vmem] * 4,
        out_specs=[vmem] * 4,
        scratch_shapes=[pltpu.VMEM((NB, NB), F32)],
        compiler_params=pltpu.CompilerParams(vmem_limit_bytes=12 * 2**20),
        cost_estimate=pl.CostEstimate(flops=SOLVE_FLOPS, bytes_accessed=0, transcendentals=0),
    )(scales, low, swap, own)


def merge_kernel(y2_ref, matrix_ref, y4_ref, y6_ref, out_ref, sem):
    del y2_ref
    prow_at = lax.axis_index("prow")
    for at, ref in ((0, matrix_ref), (4, y4_ref), (6, y6_ref)):

        @pl.when(prow_at == at)
        def _():
            copy = pltpu.make_async_copy(ref, out_ref, sem)
            copy.start()
            copy.wait()


def merge(y2, blocks):
    vmem = pl.BlockSpec(memory_space=pltpu.VMEM)
    return pl.pallas_call(
        merge_kernel,
        out_shape=pltpu.VMEM(y2.shape, BF),
        in_specs=[vmem] + [pl.BlockSpec(memory_space=pl.ANY)] * 3,
        out_specs=vmem,
        scratch_shapes=[pltpu.SemaphoreType.DMA],
        input_output_aliases={0: 0},
        compiler_params=pltpu.CompilerParams(vmem_limit_bytes=2**20),
        cost_estimate=pl.CostEstimate(flops=0, bytes_accessed=0, transcendentals=0),
    )(y2, *blocks)


def update_kernel(
    scales_ref, own_ref, even_ref, odd_ref, q0_ref, q1_ref, q3_ref, q2_ref, out_ref, result_ref, sems
):
    prow_at = lax.axis_index("prow")
    pcol_at = lax.axis_index("pcol")
    lanes = lax.broadcasted_iota(jnp.int32, (1, 2 * TILE_COLS), 1)
    own_scales = scales_ref[pl.ds(prow_at, 1), :]
    head_scales = scales_ref[:1, :]

    def pick(row, col):
        return jnp.sum(jnp.where(lanes == col, row, 0.0), axis=1, keepdims=True)

    factors = []
    for t in range(2):
        col = TILE_COLS * t + pcol_at
        value = (pick(own_scales, 0) * pick(head_scales, col)) / pick(own_scales, col)
        factors.append(jnp.broadcast_to(value, (1, NB)))
    factor = jnp.concatenate(factors, 1)
    in_panel = (lax.broadcasted_iota(jnp.int32, (1, 2 * NB), 1) < NB) & (pcol_at == 0)

    def run(head_ref):
        copies = []
        for at, (ref, shift) in enumerate(((q0_ref, 0), (q1_ref, 3), (q3_ref, 1), (q2_ref, 2))):
            rows = pl.ds(pl.multiple_of(lax.rem(pcol_at // ZS + shift, XS) * 128, 128), 128)
            product = bdot(ref[...], head_ref[...])
            own = own_ref[rows, :]
            updated = (own.astype(F32) - factor * product).astype(BF)
            result = jnp.where(prow_at == 0, product.astype(BF), updated)
            result_ref[at] = jnp.where(in_panel, own, result)
            copies.append(pltpu.make_async_copy(result_ref.at[at], out_ref.at[rows, :], sems.at[at]))
            copies[-1].start()
        for copy in copies:
            copy.wait()

    even = lax.rem(prow_at, 2) == 0
    pl.when(even)(functools.partial(run, even_ref))
    pl.when(jnp.logical_not(even))(functools.partial(run, odd_ref))


def update(scales, own, heads, chunks):
    vmem = pl.BlockSpec(memory_space=pltpu.VMEM)
    return pl.pallas_call(
        update_kernel,
        out_shape=jax.ShapeDtypeStruct((NB, 2 * NB), BF),
        in_specs=[vmem] * 8,
        out_specs=pl.BlockSpec(memory_space=pl.ANY),
        scratch_shapes=[
            pltpu.VMEM((XS, 128, 2 * NB), BF),
            pltpu.SemaphoreType.DMA((XS,)),
        ],
        compiler_params=pltpu.CompilerParams(vmem_limit_bytes=8 * 2**20),
        cost_estimate=pl.CostEstimate(flops=2**29, bytes_accessed=4 * 2**20, transcendentals=0),
    )(scales, own, *heads, *chunks)


def send(value, pairs):
    flat = [
        tuple(p * XS * ZS + x * ZS + z for p, x, z in (source, target)) for source, target in pairs
    ]
    return lax.ppermute(value, ("prow", "pcol"), flat)


def along_prow(value, pairs, columns):
    return send(value, [((a, x, z), (b, x, z)) for a, b in pairs for x, z in columns])


def along_x(value, pairs, depths):
    return send(
        value, [((p, a, z), (p, b, z)) for a, b in pairs for p in range(8) for z in depths]
    )


def along_z(value, pairs):
    return send(
        value, [((p, x, a), (p, x, b)) for a, b in pairs for p in range(8) for x in range(XS)]
    )


def on_device(matrix, scales):
    everywhere = [(x, z) for x in range(XS) for z in range(ZS)]
    corner = [(0, 0)]
    prow_at = lax.axis_index("prow")
    low = pack(matrix)
    low_y = [along_prow(low, [(0, p)], corner) for p in (2, 6, 4)]
    own, *low_y = lax.optimization_barrier((matrix, *low_y))
    low = low + low_y[0] + low_y[1] + low_y[2]
    low_swap = along_prow(low, [(p, p ^ 1) for p in range(8)], corner)
    low = jnp.where(prow_at % 2 == 0, low, 0).astype(BF)
    y2 = along_prow(own, [(0, 2)], everywhere)
    y6 = along_prow(own, [(0, 6)], everywhere)
    y4 = along_prow(own, [(0, 4)], everywhere)

    w = solve(scales, low, low_swap, matrix)
    w_x = [along_x(w[k], [(0, k)], [0]) for k in (2, 1, 3)]
    q = w[0] + w_x[0] + w_x[1] + w_x[2]
    q3, q5 = along_z(q, [(0, 3)]), along_z(q, [(0, 5)])
    q = q + q3 + q5
    q, y2, y6 = lax.optimization_barrier((q, y2, y6))
    up_z, down_z = along_z(q, [(0, 1), (3, 4), (5, 6)]), along_z(q, [(0, 7), (3, 2)])
    q = q + up_z + down_z
    q, y2, y4, y6 = lax.optimization_barrier((q, y2, y4, y6))
    even = merge(y2, (matrix, y4, y6))
    odd = along_prow(even, [(0, 1), (2, 3), (4, 5), (6, 7)], everywhere)
    q2 = along_x(q, [(a, (a + 2) % XS) for a in range(XS)], range(ZS))
    q1 = along_x(q, [(a, (a + 1) % XS) for a in range(XS)], range(ZS))
    q3 = along_x(q, [(a, (a + 3) % XS) for a in range(XS)], range(ZS))
    return update(scales, matrix, (even, odd), (q, q1, q3, q2))


def solution(mesh):
    placed = (P("prow", "pcol"), P())
    return jax.shard_map(
        on_device, mesh=mesh, in_specs=placed, out_specs=P("prow", "pcol"), check_vma=False
    )
```

```python
import functools

import jax
import jax.numpy as jnp
from jax import lax
from jax.experimental import pallas as pl
from jax.experimental.pallas import tpu as pltpu
from jax.sharding import PartitionSpec as P

NB = 512
BASE = 128
XS = 4
ZS = 8
TILE_COLS = XS * ZS
SOLVE_FLOPS = 0
BF = jnp.bfloat16
F32 = jnp.float32


def bdot(a, b):
    return jnp.dot(a, b, preferred_element_type=F32)


def split3(x):
    high = x.astype(BF)
    rest = x - high.astype(F32)
    mid = rest.astype(BF)
    low = (rest - mid.astype(F32)).astype(BF)
    return high, mid, low


def joined(left, right):
    return bdot(jnp.concatenate(left, 1), jnp.concatenate(right, 0))


def dot_exact_left(t, x):
    high, mid, low = split3(x)
    return joined([t, t], [high, mid]) + bdot(t, low)


def dot_full(a, b):
    ah, am, al = split3(a)
    bh, bm, bl = split3(b)
    return joined([ah, ah], [bh, bm]) + (
        joined([am, ah], [bh, bl]) + joined([am, al], [bm, bh])
    )


def invert_diagonal(tiles, s):
    n = BASE
    r = lax.broadcasted_iota(jnp.int32, (n, n), 0)
    c = lax.broadcasted_iota(jnp.int32, (n, n), 1)
    eye = (r == c).astype(F32)

    def mask(k):
        return ((r // (2 * k)) == (c // (2 * k))) & ((r // k) % 2 == 1) & ((c // k) % 2 == 0)

    first = mask(1)
    inverses = [eye - jnp.where(first, t.astype(F32) * s, 0.0) for t in tiles]
    k = 2
    while k < n:
        at = mask(k)
        inner = [
            dot_exact_left(jnp.where(at, t, jnp.zeros_like(t)), x) * s
            for t, x in zip(tiles, inverses)
        ]
        inverses = [x - dot_full(x, y) for x, y in zip(inverses, inner)]
        k *= 2
    return inverses


def pack_kernel(matrix_ref, out_ref, sems):
    here = (lax.axis_index("prow") == 0) & (lax.axis_index("pcol") == 0)

    @pl.when(jnp.logical_not(here))
    def _():
        out_ref[...] = jnp.zeros_like(out_ref)

    @pl.when(here)
    def _():
        pieces = [(384, 0, 128, 512, 0, 0), (256, 0, 128, 384, 128, 0), (0, 0, 128, 128, 128, 384)]
        pieces += [
            (128 + 64 * i, 128 * j, 64, 128, 256, 256 * j + 128 * i)
            for j in range(2)
            for i in range(2)
        ]
        copies = [
            pltpu.make_async_copy(
                matrix_ref.at[r : r + h, c : c + w], out_ref.at[to_r : to_r + h, to_c : to_c + w], sems.at[at]
            )
            for at, (r, c, h, w, to_r, to_c) in enumerate(pieces)
        ]
        for copy in copies:
            copy.start()
        for copy in copies:
            copy.wait()


def pack(matrix):
    return pl.pallas_call(
        pack_kernel,
        out_shape=pltpu.VMEM((320, NB), BF),
        in_specs=[pl.BlockSpec(memory_space=pl.ANY)],
        out_specs=pl.BlockSpec(memory_space=pltpu.VMEM),
        scratch_shapes=[pltpu.SemaphoreType.DMA((7,))],
        cost_estimate=pl.CostEstimate(flops=0, bytes_accessed=2**19, transcendentals=0),
    )(matrix)


def solve_kernel(
    scales_ref, low_ref, swap_ref, own_ref, w0_ref, w1_ref, w2_ref, w3_ref, inv_ref
):
    outs = (w0_ref, w1_ref, w2_ref, w3_ref)
    holder = lax.axis_index("pcol") == 0
    prow_at = lax.axis_index("prow")

    @pl.when(jnp.logical_not(holder))
    def _():
        for ref in outs:
            ref[...] = jnp.zeros_like(ref)

    @pl.when(holder)
    def _():
        s = scales_ref[:1, :1]
        packed = low_ref[...] + swap_ref[...]
        t = [[None] * 4 for _ in range(4)]
        for j in range(4):
            t[3][j] = packed[:128, 128 * j : 128 * (j + 1)]
        for j in range(3):
            t[2][j] = packed[128:256, 128 * j : 128 * (j + 1)]
        t[0][0] = packed[128:256, 384:]
        for j in range(2):
            t[1][j] = jnp.concatenate(
                [packed[256:, 256 * j : 256 * j + 128], packed[256:, 256 * j + 128 : 256 * (j + 1)]], 0
            )
        x = invert_diagonal([t[i][i] for i in range(4)], s)
        halves = []
        for h in (0, 2):
            off = -dot_full(x[h + 1], dot_exact_left(t[h + 1][h], x[h]) * s)
            top = jnp.concatenate([x[h], jnp.zeros_like(x[h])], 1)
            halves.append(jnp.concatenate([top, jnp.concatenate([off, x[h + 1]], 1)], 0))
        corner = jnp.concatenate(
            [jnp.concatenate([t[2][0], t[2][1]], 1), jnp.concatenate([t[3][0], t[3][1]], 1)], 0
        )
        off = -dot_full(halves[1], dot_exact_left(corner, halves[0]) * s)
        inv_ref[:256, :256] = halves[0]
        inv_ref[:256, 256:] = jnp.zeros_like(off)
        inv_ref[256:, :256] = off
        inv_ref[256:, 256:] = halves[1]
        inverse = inv_ref[...]
        high = inverse.astype(BF)
        low = (inverse - high.astype(F32)).astype(BF)
        for i, ref in enumerate(outs):
            a = own_ref[128 * i : 128 * (i + 1), :NB]
            w = (bdot(a, high) + bdot(a, low)).astype(BF)
            ref[...] = jnp.where(prow_at == 0, high[128 * i : 128 * (i + 1)], w)


def solve(scales, low, swap, own):
    chunk = jax.ShapeDtypeStruct((128, NB), BF)
    vmem = pl.BlockSpec(memory_space=pltpu.VMEM)
    return pl.pallas_call(
        solve_kernel,
        out_shape=[chunk] * 4,
        in_specs=[vmem] * 4,
        out_specs=[vmem] * 4,
        scratch_shapes=[pltpu.VMEM((NB, NB), F32)],
        compiler_params=pltpu.CompilerParams(vmem_limit_bytes=12 * 2**20),
        cost_estimate=pl.CostEstimate(flops=SOLVE_FLOPS, bytes_accessed=0, transcendentals=0),
    )(scales, low, swap, own)


def merge_kernel(y2_ref, matrix_ref, y4_ref, y6_ref, out_ref, sem):
    del y2_ref
    prow_at = lax.axis_index("prow")
    for at, ref in ((0, matrix_ref), (4, y4_ref), (6, y6_ref)):

        @pl.when(prow_at == at)
        def _():
            copy = pltpu.make_async_copy(ref, out_ref, sem)
            copy.start()
            copy.wait()


def merge(y2, blocks):
    vmem = pl.BlockSpec(memory_space=pltpu.VMEM)
    return pl.pallas_call(
        merge_kernel,
        out_shape=pltpu.VMEM(y2.shape, BF),
        in_specs=[vmem] + [pl.BlockSpec(memory_space=pl.ANY)] * 3,
        out_specs=vmem,
        scratch_shapes=[pltpu.SemaphoreType.DMA],
        input_output_aliases={0: 0},
        compiler_params=pltpu.CompilerParams(vmem_limit_bytes=2**20),
        cost_estimate=pl.CostEstimate(flops=0, bytes_accessed=0, transcendentals=0),
    )(y2, *blocks)


def update_kernel(
    scales_ref, own_ref, even_ref, odd_ref, q0_ref, q1_ref, q3_ref, q2_ref, out_ref, result_ref, sems
):
    prow_at = lax.axis_index("prow")
    pcol_at = lax.axis_index("pcol")
    lanes = lax.broadcasted_iota(jnp.int32, (1, 2 * TILE_COLS), 1)
    own_scales = scales_ref[pl.ds(prow_at, 1), :]
    head_scales = scales_ref[:1, :]

    def pick(row, col):
        return jnp.sum(jnp.where(lanes == col, row, 0.0), axis=1, keepdims=True)

    factors = []
    for t in range(2):
        col = TILE_COLS * t + pcol_at
        value = (pick(own_scales, 0) * pick(head_scales, col)) / pick(own_scales, col)
        factors.append(jnp.broadcast_to(value, (1, NB)))
    factor = jnp.concatenate(factors, 1)
    in_panel = (lax.broadcasted_iota(jnp.int32, (1, 2 * NB), 1) < NB) & (pcol_at == 0)

    def run(head_ref):
        copies = []
        for at, (ref, shift) in enumerate(((q0_ref, 0), (q1_ref, 3), (q3_ref, 1), (q2_ref, 2))):
            rows = pl.ds(pl.multiple_of(lax.rem(pcol_at // ZS + shift, XS) * 128, 128), 128)
            product = bdot(ref[...], head_ref[...])
            own = own_ref[rows, :]
            updated = (own.astype(F32) - factor * product).astype(BF)
            result = jnp.where(prow_at == 0, product.astype(BF), updated)
            result_ref[at] = jnp.where(in_panel, own, result)
            copies.append(pltpu.make_async_copy(result_ref.at[at], out_ref.at[rows, :], sems.at[at]))
            copies[-1].start()
        for copy in copies:
            copy.wait()

    even = lax.rem(prow_at, 2) == 0
    pl.when(even)(functools.partial(run, even_ref))
    pl.when(jnp.logical_not(even))(functools.partial(run, odd_ref))


def update(scales, own, heads, chunks):
    vmem = pl.BlockSpec(memory_space=pltpu.VMEM)
    return pl.pallas_call(
        update_kernel,
        out_shape=jax.ShapeDtypeStruct((NB, 2 * NB), BF),
        in_specs=[vmem] * 8,
        out_specs=pl.BlockSpec(memory_space=pl.ANY),
        scratch_shapes=[
            pltpu.VMEM((XS, 128, 2 * NB), BF),
            pltpu.SemaphoreType.DMA((XS,)),
        ],
        compiler_params=pltpu.CompilerParams(vmem_limit_bytes=8 * 2**20),
        cost_estimate=pl.CostEstimate(flops=2**29, bytes_accessed=4 * 2**20, transcendentals=0),
    )(scales, own, *heads, *chunks)


def send(value, pairs):
    flat = [
        tuple(p * XS * ZS + x * ZS + z for p, x, z in (source, target)) for source, target in pairs
    ]
    return lax.ppermute(value, ("prow", "pcol"), flat)


def along_prow(value, pairs, columns):
    return send(value, [((a, x, z), (b, x, z)) for a, b in pairs for x, z in columns])


def along_x(value, pairs, depths):
    return send(
        value, [((p, a, z), (p, b, z)) for a, b in pairs for p in range(8) for z in depths]
    )


def along_z(value, pairs):
    return send(
        value, [((p, x, a), (p, x, b)) for a, b in pairs for p in range(8) for x in range(XS)]
    )


def on_device(matrix, scales):
    everywhere = [(x, z) for x in range(XS) for z in range(ZS)]
    corner = [(0, 0)]
    prow_at = lax.axis_index("prow")
    low = pack(matrix)
    low_y = [along_prow(low, [(0, p)], corner) for p in (2, 6, 4)]
    own, *low_y = lax.optimization_barrier((matrix, *low_y))
    low = low + low_y[0] + low_y[1] + low_y[2]
    low_swap = along_prow(low, [(p, p ^ 1) for p in range(8)], corner)
    low = jnp.where(prow_at % 2 == 0, low, 0).astype(BF)
    y2 = along_prow(own, [(0, 2)], everywhere)
    y6 = along_prow(own, [(0, 6)], everywhere)
    y4 = along_prow(own, [(0, 4)], everywhere)

    w = solve(scales, low, low_swap, matrix)
    w_x = [along_x(w[k], [(0, k)], [0]) for k in (2, 1, 3)]
    q = w[0] + w_x[0] + w_x[1] + w_x[2]
    q3, q5 = along_z(q, [(0, 3)]), along_z(q, [(0, 5)])
    q = q + q3 + q5
    q, y2, y6 = lax.optimization_barrier((q, y2, y6))
    up_z, down_z = along_z(q, [(0, 1), (3, 4), (5, 6)]), along_z(q, [(0, 7), (3, 2)])
    q = q + up_z + down_z
    q, y2, y4, y6 = lax.optimization_barrier((q, y2, y4, y6))
    even = merge(y2, (matrix, y4, y6))
    odd = along_prow(even, [(0, 1), (2, 3), (4, 5), (6, 7)], everywhere)
    q2 = along_x(q, [(a, (a + 2) % XS) for a in range(XS)], range(ZS))
    q1 = along_x(q, [(a, (a + 1) % XS) for a in range(XS)], range(ZS))
    q3 = along_x(q, [(a, (a + 3) % XS) for a in range(XS)], range(ZS))
    return update(scales, matrix, (even, odd), (q, q1, q3, q2))


def solution(mesh):
    placed = (P("prow", "pcol"), P())
    return jax.shard_map(
        on_device, mesh=mesh, in_specs=placed, out_specs=P("prow", "pcol"), check_vma=False
    )
```
